32 devices in a mesh: sub: 4 (over z), row: 4 (over x, core), col: 2 (over y).
Axes of the slice: x: 2, y: 2, z: 4, core: 2. Of those that a mesh axis runs over, the one named last changes fastest.
Arguments:
- pressure_rhs: float32 [3, 4, 4096, 128], P(None, 'sub', 'col'), may hold values from -6 to 6
- diag_inverse: float32 [4, 4096, 7, 4096], P('sub', 'row', None, 'col'), as said below
- factor_blocks: float32 [3, 4, 2048, 4096], P(None, 'sub', 'col', 'row'), may hold values from -0.09375 to 0.09375
- row_lists: int32 [3, 4, 2048], P(None, 'sub', 'col'), may hold values from 0 to 16383, as said below
Outputs:
- solution: float32 [3, 4, 4096, 128], P(None, 'sub', 'col')
The draws below stay inside these ranges and needn't reach their ends.
Inputs may be any that keep to these rules, and one draw needn't show every extreme that they name: `diag_inverse`: in slot 2^l - 1 + q the block of row panel s is zero where q > s mod 2^l, and lower triangular with diagonal entries between 0.5 and 2 where q = s mod 2^l. row_lists[t, s, k] = q * 4096 + 2 k + e with e 0 or 1 and q below 2^m, m the upper level of pair t; entry 0 of every list is 0 and entry 2047 is 2^m * 4096 - 1.
All inputs are finite; a program needn't handle non-finite values.
Results may differ from the reference program's by a relative error of at most 0.00012.
Values sent between devices are 32-bit elements; how exact they have to be, the bound alone decides.
A program may use at most 192 MiB of HBM per device.

```python
import jax
import jax.numpy as jnp
import numpy as np
from jax import lax

S = 4096
NRHS = 128
K = 2048
PANELS = 4
LEVELS = 3
SLOTS = 7
PAIRS = 3


def level_of_slot(slot_ids):
    level_ids = jnp.zeros_like(slot_ids)
    for power in range(1, (2 * PANELS).bit_length()):
        level_ids = level_ids + (slot_ids + 1 >= 2 ** power).astype(jnp.int32)
    return level_ids


def draw_diag_inverse(key, part):
    key_noise, key_diag = jax.random.split(key)
    slot_ids = jnp.arange(SLOTS, dtype=jnp.int32)
    level_ids = level_of_slot(slot_ids)
    span_sizes = jnp.left_shift(jnp.int32(1), level_ids)
    column_panel = slot_ids + 1 - span_sizes
    panel_ids = jnp.arange(PANELS, dtype=jnp.int32)
    row_panel = panel_ids[:, None] % span_sizes[None, :]
    dense_part = (column_panel[None, :] < row_panel)[:, None, :, None]
    on_block = (column_panel[None, :] == row_panel)[:, None, :, None]
    shape = (PANELS, S, SLOTS, S)
    noise = jax.random.normal(key_noise, shape, jnp.float32)
    diag_values = jnp.exp(jax.random.uniform(key_diag, (PANELS, S, SLOTS, 1), jnp.float32, -0.6931472, 0.6931472))
    row_ids = jnp.arange(S, dtype=jnp.int32)
    strict_lower = (row_ids[:, None] > row_ids[None, :])[None, :, None, :]
    on_diag = (row_ids[:, None] == row_ids[None, :])[None, :, None, :]
    far_scale = (0.8 / jnp.sqrt(span_sizes.astype(jnp.float32) * S))[None, None, :, None]
    near_values = jnp.where(strict_lower, noise * (0.7 / np.sqrt(S)), 0.0) + jnp.where(on_diag, diag_values, 0.0)
    far_values = noise * far_scale
    return jnp.where(on_block, near_values, jnp.where(dense_part, far_values, 0.0)).astype(jnp.float32)


def draw_row_lists(key, part):
    upper_levels = []
    for low_level in range(LEVELS):
        for high_level in range(low_level + 1, LEVELS):
            upper_levels.append(high_level)
    upper_table = jnp.asarray(np.array(upper_levels, dtype=np.int32))
    span_sizes = jnp.left_shift(jnp.int32(1), upper_table)[:, None, None]
    key_panel, key_parity = jax.random.split(key)
    panel_pick = jax.random.randint(key_panel, (PAIRS, PANELS, K), 0, 1 << 20, dtype=jnp.int32) % span_sizes
    parity = jax.random.randint(key_parity, (PAIRS, PANELS, K), 0, 2, dtype=jnp.int32)
    entry_ids = jnp.arange(K, dtype=jnp.int32)[None, None, :]
    panel_pick = jnp.where(entry_ids == 0, 0, jnp.where(entry_ids == K - 1, span_sizes - 1, panel_pick))
    parity = jnp.where(entry_ids == 0, 0, jnp.where(entry_ids == K - 1, 1, parity))
    return (panel_pick * S + 2 * entry_ids + parity).astype(jnp.int32)


def steps_of(stream_key, dims, shards, smallest, largest):
    factor_of, own = 1.0, jax.random.fold_in(stream_key, 6)
    for axis_at, shards_of in shards:
        draws = jnp.exp(jax.random.uniform(jax.random.fold_in(own, axis_at), (shards_of,), jnp.float32, smallest / len(shards), largest / len(shards)))
        factor_of = factor_of * jnp.repeat(draws, dims[axis_at] // shards_of).reshape([-1 if axis == axis_at else 1 for axis in range(len(dims))])
    return factor_of


def centred(own_key, dims, width, most, cuts=(), held_as=jnp.bfloat16):
    loudness = steps_of(own_key, dims, cuts, -0.22, 0.18) if cuts else 1.0
    result = jax.random.normal(own_key, dims, jnp.float32) * width * loudness
    return jnp.minimum(jnp.maximum(result, -most), most).astype(held_as)


def setup_inputs(seed: int = 0) -> dict:
    streams_of = jax.random.split(jax.random.key(seed), 5)
    return {
        "pressure_rhs": centred(streams_of[0], (LEVELS, PANELS, S, NRHS), 1.0, 6.0, ((1, 4), (2, 2)), jnp.float32),
        "diag_inverse": draw_diag_inverse(jax.random.fold_in(streams_of[4], 71), 0),
        "factor_blocks": centred(streams_of[2], (PAIRS, PANELS, K, S), S ** -0.5, 0.09375, ((1, 4), (2, 2), (3, 4)), jnp.float32),
        "row_lists": draw_row_lists(jax.random.fold_in(streams_of[4], 71), 0),
    }


exact_mode = lax.Precision.HIGHEST


def pair_slot(low_level, high_level):
    return low_level * (LEVELS - 1) - low_level * (low_level - 1) // 2 + high_level - low_level - 1


def target_rows(row_lists, low_level, high_level):
    span_size = 2 ** high_level
    base_rows = (jnp.arange(PANELS, dtype=jnp.int32) // span_size) * (span_size * S)
    return (base_rows[:, None] + row_lists[pair_slot(low_level, high_level)]).astype(jnp.int32)


def reference(pressure_rhs, diag_inverse, factor_blocks, row_lists):
    totals = [jnp.zeros((PANELS * S, NRHS), jnp.float32) for level_num in range(LEVELS)]
    solved = []
    for level_num in range(LEVELS):
        span_size = 2 ** level_num
        right_side = pressure_rhs[level_num] - totals[level_num].reshape(PANELS, S, NRHS)
        diag_blocks = diag_inverse[:, :, span_size - 1:2 * span_size - 1, :]
        grouped = right_side.reshape(PANELS // span_size, span_size, S, NRHS)
        spread_rhs = jnp.repeat(grouped, span_size, axis=0)
        solved_level = jnp.einsum("pias,pasn->pin", diag_blocks, spread_rhs, precision=exact_mode)
        solved.append(solved_level)
        for high_level in range(level_num + 1, LEVELS):
            slot_index = pair_slot(level_num, high_level)
            update_rows = jnp.einsum("pks,psn->pkn", factor_blocks[slot_index], solved_level, precision=exact_mode)
            where_to = target_rows(row_lists, level_num, high_level).reshape(-1)
            totals[high_level] = totals[high_level].at[where_to].add(update_rows.reshape(-1, NRHS))
    results = [None] * LEVELS
    for level_num in reversed(range(LEVELS)):
        span_size = 2 ** level_num
        residue = solved[level_num]
        for high_level in range(level_num + 1, LEVELS):
            slot_index = pair_slot(level_num, high_level)
            where_from = target_rows(row_lists, level_num, high_level)
            picked = results[high_level].reshape(PANELS * S, NRHS)[where_from]
            residue = residue - jnp.einsum("pks,pkn->psn", factor_blocks[slot_index], picked, precision=exact_mode)
        diag_blocks = diag_inverse[:, :, span_size - 1:2 * span_size - 1, :]
        pieces = jnp.einsum("pias,pin->pasn", diag_blocks, residue, precision=exact_mode)
        summed = pieces.reshape(PANELS // span_size, span_size, span_size, S, NRHS).sum(axis=1)
        results[level_num] = summed.reshape(PANELS, S, NRHS)
    return jnp.stack(results)
```

```python
import functools

import jax
import jax.numpy as jnp
from jax import lax
from jax.experimental import pallas as pl
from jax.experimental.pallas import tpu as pltpu
from jax.sharding import PartitionSpec as P

dot_mode = lax.Precision.HIGH
VMEM = pl.BlockSpec(memory_space=pltpu.VMEM)
VMEM_BYTES = 40 * 2**20


def greet(devices):
    barrier = pltpu.get_barrier_semaphore()
    for device in devices:
        pl.semaphore_signal(
            barrier, inc=1, device_id=device, device_id_type=pl.DeviceIdType.MESH
        )
    pl.semaphore_wait(barrier, len(devices))


def remote(source, target, sends, recvs, at, device):
    return pltpu.make_async_remote_copy(
        src_ref=source,
        dst_ref=target,
        send_sem=sends.at[at],
        recv_sem=recvs.at[at],
        device_id=device,
        device_id_type=pl.DeviceIdType.MESH,
    )


def row_peers():
    me = lax.axis_index("row")
    near = me + 1 - 2 * (me % 2)
    far = (me + 2) % 4
    return me, near, far


def row_scatter_kernel(count, x_ref, out_ref, near_in, far_out, far_in, sends, recvs):
    me, near, far = row_peers()
    core, chip = me % 2, me // 2
    greet([{"row": near}, {"row": far}])
    hops = []
    for q in range(count):
        for j, block in enumerate((1 - chip, chip)):
            hop = remote(
                x_ref.at[q, 2 * block + 1 - core], near_in.at[q, j],
                sends, recvs, 3 * q + j, {"row": near},
            )
            hop.start()
            hops.append(hop)
    links = []
    for q in range(count):
        hops[2 * q].wait_recv()
        far_out[q] = x_ref[q, 2 * (1 - chip) + core] + near_in[q, 0]
        link = remote(far_out.at[q], far_in.at[q], sends, recvs, 3 * q + 2, {"row": far})
        link.start()
        links.append(link)
    for q in range(count):
        hops[2 * q + 1].wait_recv()
        links[q].wait_recv()
        out_ref[q] = x_ref[q, me] + near_in[q, 1] + far_in[q]
    for copy in hops + links:
        copy.wait_send()


def row_gather_kernel(count, x_ref, out_ref, sends, recvs):
    me, near, far = row_peers()
    across = (near + 2) % 4
    greet([{"row": near}, {"row": far}])
    started = []
    for q in range(count):
        for j, device in enumerate((far, near)):
            copy = remote(
                x_ref.at[q], out_ref.at[q, me], sends, recvs, 3 * q + j, {"row": device}
            )
            copy.start()
            started.append(copy)
    for q in range(count):
        out_ref[q, me] = x_ref[q]
    for q in range(count):
        remote(
            x_ref.at[q], out_ref.at[q, far], sends, recvs, 3 * q, {"row": far}
        ).wait_recv()
        copy = remote(
            out_ref.at[q, far], out_ref.at[q, far], sends, recvs, 3 * q + 2, {"row": near}
        )
        copy.start()
        started.append(copy)
    for q in range(count):
        remote(
            x_ref.at[q], out_ref.at[q, near], sends, recvs, 3 * q + 1, {"row": near}
        ).wait_recv()
        remote(
            x_ref.at[q], out_ref.at[q, across], sends, recvs, 3 * q + 2, {"row": near}
        ).wait_recv()
    for copy in started:
        copy.wait_send()


def sub_peers(span_size):
    me = lax.axis_index("sub")
    place = me % span_size
    base = me - place
    ahead = [(place + d) % span_size for d in range(1, span_size)]
    behind = [(place + span_size - d) % span_size for d in range(1, span_size)]
    return place, base, ahead, behind


def sub_gather_kernel(span_size, x_ref, out_ref, sends, recvs):
    place, base, ahead, behind = sub_peers(span_size)
    greet([{"sub": base + to} for to in ahead])
    started = []
    for d, to in enumerate(ahead):
        copy = remote(x_ref, out_ref.at[place], sends, recvs, d, {"sub": base + to})
        copy.start()
        started.append(copy)
    out_ref[place] = x_ref[...]
    for d, origin in enumerate(behind):
        remote(
            x_ref, out_ref.at[origin], sends, recvs, d, {"sub": base + ahead[d]}
        ).wait_recv()
    for copy in started:
        copy.wait_send()


def sub_scatter_kernel(span_size, x_ref, out_ref, landing, sends, recvs):
    place, base, ahead, _ = sub_peers(span_size)
    greet([{"sub": base + to} for to in ahead])
    started = []
    for d, to in enumerate(ahead):
        copy = remote(
            x_ref.at[to], landing.at[d], sends, recvs, d, {"sub": base + to}
        )
        copy.start()
        started.append(copy)
    total = x_ref[place]
    for d, copy in enumerate(started):
        copy.wait_recv()
        total = total + landing[d]
    out_ref[...] = total
    for copy in started:
        copy.wait_send()


call_ids = {}


def exchange(kind, kernel, x, out_dims, scratch, copies):
    key = (kind, x.shape)
    call_id = call_ids.setdefault(key, len(call_ids))
    return pl.pallas_call(
        kernel,
        out_shape=jax.ShapeDtypeStruct(out_dims, jnp.float32),
        in_specs=[VMEM],
        out_specs=VMEM,
        scratch_shapes=[pltpu.VMEM(dims, jnp.float32) for dims in scratch]
        + [pltpu.SemaphoreType.DMA((copies,))] * 2,
        compiler_params=pltpu.CompilerParams(
            collective_id=call_id, has_side_effects=True, vmem_limit_bytes=VMEM_BYTES
        ),
        cost_estimate=pl.CostEstimate(
            flops=0, bytes_accessed=20 * x.size, transcendentals=0
        ),
    )(x)


def row_scatter(values):
    count, rows, width = values.shape
    share = rows // 4
    return exchange(
        "row_scatter",
        functools.partial(row_scatter_kernel, count),
        values.reshape(count, 4, share, width),
        (count, share, width),
        [(count, 2, share, width), (count, share, width), (count, share, width)],
        3 * count,
    )


def row_gather(values):
    count, share, width = values.shape
    return exchange(
        "row_gather",
        functools.partial(row_gather_kernel, count),
        values,
        (count, 4, share, width),
        [],
        3 * count,
    ).reshape(count, 4 * share, width)


def group_gather(values, level_num):
    span_size = 2**level_num
    return exchange(
        "sub_gather" + str(span_size),
        functools.partial(sub_gather_kernel, span_size),
        values,
        (span_size,) + values.shape,
        [],
        span_size - 1,
    )


def group_scatter(values, level_num):
    span_size = 2**level_num
    if span_size == 1:
        return values[0]
    return exchange(
        "sub_scatter" + str(span_size),
        functools.partial(sub_scatter_kernel, span_size),
        values,
        values.shape[1:],
        [(span_size - 1,) + values.shape[1:]],
        span_size - 1,
    )


def swapped(value, axis, bit):
    mask = 2**bit
    pairs = [(source, source ^ mask) for source in range(lax.axis_size(axis))]
    return lax.ppermute(value, axis, pairs)


def col_total(values):
    if lax.axis_size("col") == 2:
        return values + swapped(values, "col", 0)
    return lax.psum(values, "col")


def pair_slot(low_level, high_level, level_count):
    return (
        low_level * (level_count - 1)
        - low_level * (low_level - 1) // 2
        + high_level
        - low_level
        - 1
    )


def early_gather(values, level_num):
    span_size = 2**level_num
    if span_size == lax.axis_size("sub"):
        return lax.all_gather(values, "sub")
    place = lax.axis_index("sub") % span_size
    blocks = values[None]
    for bit in range(level_num):
        other = swapped(blocks, "sub", bit)
        first = ((place >> bit) & 1) == 0
        blocks = jnp.concatenate(
            [jnp.where(first, blocks, other), jnp.where(first, other, blocks)]
        )
    return blocks


def expand_kernel(span_size, chunk, rhs_ref, up_ref, code_ref, out_ref):
    rows = up_ref.shape[1]

    @pl.loop(0, rows // chunk)
    def _(step):
        first = pl.multiple_of(step * chunk, chunk)
        here = pl.ds(first, chunk)
        for panel in range(span_size):
            for parity in range(2):
                total = jnp.zeros((chunk, up_ref.shape[2]), jnp.float32)
                for source in range(span_size):
                    total = total + jnp.where(
                        code_ref[source, here] == 2 * panel + parity,
                        up_ref[source, here],
                        0.0,
                    )
                there = pl.ds(2 * first + parity, chunk, stride=2)
                out_ref[panel, there, :] = rhs_ref[panel, there, :] - total


def minus_expanded(rhs, updates, codes):
    span_size = updates.shape[0]
    wide = jnp.broadcast_to(codes[:, :, None], updates.shape)
    return pl.pallas_call(
        functools.partial(expand_kernel, span_size, min(64, updates.shape[1])),
        out_shape=jax.ShapeDtypeStruct(rhs.shape, jnp.float32),
        in_specs=[VMEM] * 3,
        out_specs=VMEM,
        compiler_params=pltpu.CompilerParams(vmem_limit_bytes=VMEM_BYTES),
    )(rhs, updates, wide)


def pick_kernel(span_size, low_count, x_ref, mark_ref, out_ref):
    rows = mark_ref.shape[2]
    even = x_ref[pl.ds(0, rows, stride=2), :]
    odd = x_ref[pl.ds(1, rows, stride=2), :]
    for to in range(span_size):
        for low in range(low_count):
            mark = mark_ref[to, low]
            out_ref[to, low] = jnp.where(mark == 0, even, jnp.where(mark == 1, odd, 0.0))


def picks(own_share, marks):
    span_size, low_count, rows = marks.shape
    dims = marks.shape + own_share.shape[1:]
    wide = jnp.broadcast_to(marks[..., None], dims)
    return pl.pallas_call(
        functools.partial(pick_kernel, span_size, low_count),
        out_shape=jax.ShapeDtypeStruct(dims, jnp.float32),
        in_specs=[VMEM] * 2,
        out_specs=VMEM,
        compiler_params=pltpu.CompilerParams(vmem_limit_bytes=VMEM_BYTES),
    )(own_share, wide)


def on_device(pressure_rhs, diag_inverse, factor_blocks, row_lists):
    level_count = pressure_rhs.shape[0]
    panel_rows = pressure_rhs.shape[2] * lax.axis_size("col")
    list_rows = row_lists.shape[2]
    share_rows = list_rows // lax.axis_size("row")
    sub_at = lax.axis_index("sub")
    row_at = lax.axis_index("row")

    lists = row_lists[:, 0]
    codes = lists // panel_rows * 2 + lists % 2
    all_codes = lax.all_gather(codes, "sub")

    def codes_of(slot_index, level_num):
        span_size = 2**level_num
        base = sub_at // span_size * span_size
        return lax.dynamic_slice_in_dim(all_codes[:, slot_index], base, span_size, 0)

    rhs = {}
    for level_num in range(1, level_count):
        rhs[level_num] = early_gather(pressure_rhs[level_num, 0], level_num)

    solved = []
    for level_num in range(level_count):
        span_size = 2**level_num
        gathered = rhs[level_num] if level_num else pressure_rhs[0]
        diag_blocks = diag_inverse[0, :, span_size - 1 : 2 * span_size - 1, :]
        column_part = jnp.einsum("ias,asn->in", diag_blocks, gathered, precision=dot_mode)
        solved_panel = col_total(column_part)
        if level_num + 1 < level_count:
            solved_panel, rhs[level_num + 1] = lax.optimization_barrier(
                (solved_panel, rhs[level_num + 1])
            )
        solved.append(solved_panel)
        for high_level in range(level_num + 1, level_count):
            slot_index = pair_slot(level_num, high_level, level_count)
            part = jnp.dot(factor_blocks[slot_index, 0], solved_panel, precision=dot_mode)
            share = row_scatter(part[None])[0]
            shares = group_gather(share, high_level)
            updates = row_gather(shares)
            rhs[high_level] = minus_expanded(
                rhs[high_level], updates, codes_of(slot_index, high_level)
            )

    picked = {}
    outputs = [None] * level_count
    for level_num in reversed(range(level_count)):
        span_size = 2**level_num
        place = sub_at % span_size
        residue = solved[level_num]
        if level_num < level_count - 1:
            correction = 0.0
            for high_level in reversed(range(level_num + 1, level_count)):
                slot_index = pair_slot(level_num, high_level, level_count)
                correction = correction + jnp.einsum(
                    "ks,kn->sn",
                    factor_blocks[slot_index, 0],
                    picked[level_num, high_level],
                    precision=dot_mode,
                )
            residue = residue - col_total(correction)
            if level_num == 0:
                late = [outputs[high] for high in range(1, level_count)]
                residue, outputs[1:] = lax.optimization_barrier((residue, late))
        diag_blocks = diag_inverse[0, :, span_size - 1 : 2 * span_size - 1, :]
        pieces = jnp.einsum("ias,in->asn", diag_blocks, residue, precision=dot_mode)
        shares = row_scatter(pieces)
        own_share = group_scatter(shares, level_num)
        if level_num:
            marks = []
            for low_level in range(level_num):
                slot_index = pair_slot(low_level, level_num, level_count)
                marks.append(
                    lax.dynamic_slice_in_dim(
                        codes_of(slot_index, level_num), row_at * share_rows, share_rows, 1
                    )
                    - 2 * place
                )
            sums = group_scatter(picks(own_share, jnp.stack(marks, axis=1)), level_num)
            full = row_gather(sums)
            for low_level in range(level_num):
                picked[low_level, level_num] = full[low_level]
        if level_num:
            outputs[level_num] = lax.all_gather(own_share, "row", axis=0, tiled=True)
        else:
            outputs[level_num] = row_gather(own_share[None])[0]
    return jnp.stack(outputs)[:, None]


def solution(mesh):
    in_specs = (
        P(None, "sub", "col", None),
        P("sub", "row", None, "col"),
        P(None, "sub", "col", "row"),
        P(None, "sub", "col"),
    )
    out_specs = P(None, "sub", "col", None)
    return jax.shard_map(
        on_device, mesh=mesh, in_specs=in_specs, out_specs=out_specs, check_vma=False
    )
```

```python
import functools

import jax
import jax.numpy as jnp
from jax import lax
from jax.experimental import pallas as pl
from jax.experimental.pallas import tpu as pltpu
from jax.sharding import PartitionSpec as P

dot_mode = lax.Precision.HIGH
VMEM = pl.BlockSpec(memory_space=pltpu.VMEM)
VMEM_BYTES = 40 * 2**20


def greet(devices):
    barrier = pltpu.get_barrier_semaphore()
    for device in devices:
        pl.semaphore_signal(
            barrier, inc=1, device_id=device, device_id_type=pl.DeviceIdType.MESH
        )
    pl.semaphore_wait(barrier, len(devices))


def remote(source, target, sends, recvs, at, device):
    return pltpu.make_async_remote_copy(
        src_ref=source,
        dst_ref=target,
        send_sem=sends.at[at],
        recv_sem=recvs.at[at],
        device_id=device,
        device_id_type=pl.DeviceIdType.MESH,
    )


def row_peers():
    me = lax.axis_index("row")
    near = me + 1 - 2 * (me % 2)
    far = (me + 2) % 4
    return me, near, far


def row_scatter_kernel(count, x_ref, out_ref, near_in, far_out, far_in, sends, recvs):
    me, near, far = row_peers()
    core, chip = me % 2, me // 2
    greet([{"row": near}, {"row": far}])
    hops = []
    for q in range(count):
        for j, block in enumerate((1 - chip, chip)):
            hop = remote(
                x_ref.at[q, 2 * block + 1 - core], near_in.at[q, j],
                sends, recvs, 3 * q + j, {"row": near},
            )
            hop.start()
            hops.append(hop)
    links = []
    for q in range(count):
        hops[2 * q].wait_recv()
        far_out[q] = x_ref[q, 2 * (1 - chip) + core] + near_in[q, 0]
        link = remote(far_out.at[q], far_in.at[q], sends, recvs, 3 * q + 2, {"row": far})
        link.start()
        links.append(link)
    for q in range(count):
        hops[2 * q + 1].wait_recv()
        links[q].wait_recv()
        out_ref[q] = x_ref[q, me] + near_in[q, 1] + far_in[q]
    for copy in hops + links:
        copy.wait_send()


def row_gather_kernel(count, x_ref, out_ref, sends, recvs):
    me, near, far = row_peers()
    across = (near + 2) % 4
    greet([{"row": near}, {"row": far}])
    started = []
    for q in range(count):
        for j, device in enumerate((far, near)):
            copy = remote(
                x_ref.at[q], out_ref.at[q, me], sends, recvs, 3 * q + j, {"row": device}
            )
            copy.start()
            started.append(copy)
    for q in range(count):
        out_ref[q, me] = x_ref[q]
    for q in range(count):
        remote(
            x_ref.at[q], out_ref.at[q, far], sends, recvs, 3 * q, {"row": far}
        ).wait_recv()
        copy = remote(
            out_ref.at[q, far], out_ref.at[q, far], sends, recvs, 3 * q + 2, {"row": near}
        )
        copy.start()
        started.append(copy)
    for q in range(count):
        remote(
            x_ref.at[q], out_ref.at[q, near], sends, recvs, 3 * q + 1, {"row": near}
        ).wait_recv()
        remote(
            x_ref.at[q], out_ref.at[q, across], sends, recvs, 3 * q + 2, {"row": near}
        ).wait_recv()
    for copy in started:
        copy.wait_send()


def sub_peers(span_size):
    me = lax.axis_index("sub")
    place = me % span_size
    base = me - place
    ahead = [(place + d) % span_size for d in range(1, span_size)]
    behind = [(place + span_size - d) % span_size for d in range(1, span_size)]
    return place, base, ahead, behind


def sub_gather_kernel(span_size, x_ref, out_ref, sends, recvs):
    place, base, ahead, behind = sub_peers(span_size)
    greet([{"sub": base + to} for to in ahead])
    started = []
    for d, to in enumerate(ahead):
        copy = remote(x_ref, out_ref.at[place], sends, recvs, d, {"sub": base + to})
        copy.start()
        started.append(copy)
    out_ref[place] = x_ref[...]
    for d, origin in enumerate(behind):
        remote(
            x_ref, out_ref.at[origin], sends, recvs, d, {"sub": base + ahead[d]}
        ).wait_recv()
    for copy in started:
        copy.wait_send()


def sub_scatter_kernel(span_size, x_ref, out_ref, landing, sends, recvs):
    place, base, ahead, _ = sub_peers(span_size)
    greet([{"sub": base + to} for to in ahead])
    started = []
    for d, to in enumerate(ahead):
        copy = remote(
            x_ref.at[to], landing.at[d], sends, recvs, d, {"sub": base + to}
        )
        copy.start()
        started.append(copy)
    total = x_ref[place]
    for d, copy in enumerate(started):
        copy.wait_recv()
        total = total + landing[d]
    out_ref[...] = total
    for copy in started:
        copy.wait_send()


call_ids = {}


def exchange(kind, kernel, x, out_dims, scratch, copies):
    key = (kind, x.shape)
    call_id = call_ids.setdefault(key, len(call_ids))
    return pl.pallas_call(
        kernel,
        out_shape=jax.ShapeDtypeStruct(out_dims, jnp.float32),
        in_specs=[VMEM],
        out_specs=VMEM,
        scratch_shapes=[pltpu.VMEM(dims, jnp.float32) for dims in scratch]
        + [pltpu.SemaphoreType.DMA((copies,))] * 2,
        compiler_params=pltpu.CompilerParams(
            collective_id=call_id, has_side_effects=True, vmem_limit_bytes=VMEM_BYTES
        ),
        cost_estimate=pl.CostEstimate(
            flops=0, bytes_accessed=20 * x.size, transcendentals=0
        ),
    )(x)


def row_scatter(values):
    count, rows, width = values.shape
    share = rows // 4
    return exchange(
        "row_scatter",
        functools.partial(row_scatter_kernel, count),
        values.reshape(count, 4, share, width),
        (count, share, width),
        [(count, 2, share, width), (count, share, width), (count, share, width)],
        3 * count,
    )


def row_gather(values):
    count, share, width = values.shape
    return exchange(
        "row_gather",
        functools.partial(row_gather_kernel, count),
        values,
        (count, 4, share, width),
        [],
        3 * count,
    ).reshape(count, 4 * share, width)


def group_gather(values, level_num):
    span_size = 2**level_num
    return exchange(
        "sub_gather" + str(span_size),
        functools.partial(sub_gather_kernel, span_size),
        values,
        (span_size,) + values.shape,
        [],
        span_size - 1,
    )


def group_scatter(values, level_num):
    span_size = 2**level_num
    if span_size == 1:
        return values[0]
    return exchange(
        "sub_scatter" + str(span_size),
        functools.partial(sub_scatter_kernel, span_size),
        values,
        values.shape[1:],
        [(span_size - 1,) + values.shape[1:]],
        span_size - 1,
    )


def swapped(value, axis, bit):
    mask = 2**bit
    pairs = [(source, source ^ mask) for source in range(lax.axis_size(axis))]
    return lax.ppermute(value, axis, pairs)


def col_total(values):
    if lax.axis_size("col") == 2:
        return values + swapped(values, "col", 0)
    return lax.psum(values, "col")


def pair_slot(low_level, high_level, level_count):
    return (
        low_level * (level_count - 1)
        - low_level * (low_level - 1) // 2
        + high_level
        - low_level
        - 1
    )


def shifted(value):
    count = lax.axis_size("sub")
    return lax.ppermute(value, "sub", [(at, at + 1) for at in range(count - 1)])


def in_place_order(steps):
    span_size = len(steps)
    place = lax.axis_index("sub") % span_size
    panels = []
    for panel in range(span_size):
        chosen = steps[0]
        for d in range(1, span_size):
            chosen = jnp.where(place - panel == d, steps[d], chosen)
        panels.append(chosen)
    return jnp.stack(panels)


def expand_kernel(span_size, chunk, rhs_ref, up_ref, code_ref, out_ref):
    rows = up_ref.shape[1]

    @pl.loop(0, rows // chunk)
    def _(step):
        first = pl.multiple_of(step * chunk, chunk)
        here = pl.ds(first, chunk)
        for panel in range(span_size):
            for parity in range(2):
                total = jnp.zeros((chunk, up_ref.shape[2]), jnp.float32)
                for source in range(span_size):
                    total = total + jnp.where(
                        code_ref[source, here] == 2 * panel + parity,
                        up_ref[source, here],
                        0.0,
                    )
                there = pl.ds(2 * first + parity, chunk, stride=2)
                out_ref[panel, there, :] = rhs_ref[panel, there, :] - total


def minus_expanded(rhs, updates, codes):
    span_size = updates.shape[0]
    wide = jnp.broadcast_to(codes[:, :, None], updates.shape)
    return pl.pallas_call(
        functools.partial(expand_kernel, span_size, min(64, updates.shape[1])),
        out_shape=jax.ShapeDtypeStruct(rhs.shape, jnp.float32),
        in_specs=[VMEM] * 3,
        out_specs=VMEM,
        compiler_params=pltpu.CompilerParams(vmem_limit_bytes=VMEM_BYTES),
    )(rhs, updates, wide)


def pick_kernel(span_size, low_count, x_ref, mark_ref, out_ref):
    rows = mark_ref.shape[2]
    even = x_ref[pl.ds(0, rows, stride=2), :]
    odd = x_ref[pl.ds(1, rows, stride=2), :]
    for to in range(span_size):
        for low in range(low_count):
            mark = mark_ref[to, low]
            out_ref[to, low] = jnp.where(mark == 0, even, jnp.where(mark == 1, odd, 0.0))


def picks(own_share, marks):
    span_size, low_count, rows = marks.shape
    dims = marks.shape + own_share.shape[1:]
    wide = jnp.broadcast_to(marks[..., None], dims)
    return pl.pallas_call(
        functools.partial(pick_kernel, span_size, low_count),
        out_shape=jax.ShapeDtypeStruct(dims, jnp.float32),
        in_specs=[VMEM] * 2,
        out_specs=VMEM,
        compiler_params=pltpu.CompilerParams(vmem_limit_bytes=VMEM_BYTES),
    )(own_share, wide)


def on_device(pressure_rhs, diag_inverse, factor_blocks, row_lists):
    level_count = pressure_rhs.shape[0]
    panel_rows = pressure_rhs.shape[2] * lax.axis_size("col")
    list_rows = row_lists.shape[2]
    share_rows = list_rows // lax.axis_size("row")
    sub_at = lax.axis_index("sub")
    row_at = lax.axis_index("row")

    lists = row_lists[:, 0]
    codes = lists // panel_rows * 2 + lists % 2
    all_codes = lax.all_gather(codes, "sub")

    def codes_of(slot_index, level_num):
        span_size = 2**level_num
        base = sub_at // span_size * span_size
        return lax.dynamic_slice_in_dim(all_codes[:, slot_index], base, span_size, 0)

    steps = {m: [pressure_rhs[m, 0]] for m in range(1, level_count)}
    steps[1].append(shifted(steps[1][0]))

    def hop_after(level_num, ready):
        value, _ = lax.optimization_barrier((steps[level_num][-1], ready))
        steps[level_num].append(shifted(value))

    rhs = {}
    waiting = {m: [] for m in range(1, level_count)}
    solved = []
    for level_num in range(level_count):
        span_size = 2**level_num
        gathered = pressure_rhs[0]
        if level_num:
            gathered = rhs[level_num]
            for updates, codes_here in waiting[level_num]:
                gathered = minus_expanded(gathered, updates, codes_here)
            if level_num + 1 < level_count:
                hop_after(level_num + 1, gathered)
        diag_blocks = diag_inverse[0, :, span_size - 1 : 2 * span_size - 1, :]
        column_part = jnp.einsum("ias,asn->in", diag_blocks, gathered, precision=dot_mode)
        solved_panel = col_total(column_part)
        if level_num + 1 < level_count:
            early = steps[level_num + 1]
            solved_panel, early = lax.optimization_barrier((solved_panel, early))
            steps[level_num + 1] = list(early)
            while len(steps[level_num + 1]) < 2 ** (level_num + 1):
                hop_after(level_num + 1, solved_panel)
            rhs[level_num + 1] = in_place_order(steps[level_num + 1])
            if level_num + 2 < level_count:
                hop_after(level_num + 2, solved_panel)
        solved.append(solved_panel)
        for high_level in range(level_num + 1, level_count):
            slot_index = pair_slot(level_num, high_level, level_count)
            part = jnp.dot(factor_blocks[slot_index, 0], solved_panel, precision=dot_mode)
            share = row_scatter(part[None])[0]
            shares = group_gather(share, high_level)
            updates = row_gather(shares)
            waiting[high_level].append((updates, codes_of(slot_index, high_level)))

    picked = {}
    outputs = [None] * level_count
    for level_num in reversed(range(level_count)):
        span_size = 2**level_num
        place = sub_at % span_size
        residue = solved[level_num]
        if level_num < level_count - 1:
            correction = 0.0
            for high_level in reversed(range(level_num + 1, level_count)):
                slot_index = pair_slot(level_num, high_level, level_count)
                correction = correction + jnp.einsum(
                    "ks,kn->sn",
                    factor_blocks[slot_index, 0],
                    picked[level_num, high_level],
                    precision=dot_mode,
                )
            residue = residue - col_total(correction)
            if level_num == 0:
                late = [outputs[high] for high in range(1, level_count)]
                residue, outputs[1:] = lax.optimization_barrier((residue, late))
        diag_blocks = diag_inverse[0, :, span_size - 1 : 2 * span_size - 1, :]
        pieces = jnp.einsum("ias,in->asn", diag_blocks, residue, precision=dot_mode)
        shares = row_scatter(lax.optimization_barrier(pieces))
        own_share = group_scatter(shares, level_num)
        if level_num:
            marks = []
            for low_level in range(level_num):
                slot_index = pair_slot(low_level, level_num, level_count)
                marks.append(
                    lax.dynamic_slice_in_dim(
                        codes_of(slot_index, level_num), row_at * share_rows, share_rows, 1
                    )
                    - 2 * place
                )
            sums = group_scatter(picks(own_share, jnp.stack(marks, axis=1)), level_num)
            full = row_gather(sums)
            for low_level in range(level_num):
                picked[low_level, level_num] = full[low_level]
        if level_num:
            outputs[level_num] = lax.all_gather(own_share, "row", axis=0, tiled=True)
        else:
            outputs[level_num] = row_gather(own_share[None])[0]
    return jnp.stack(outputs)[:, None]


def solution(mesh):
    in_specs = (
        P(None, "sub", "col", None),
        P("sub", "row", None, "col"),
        P(None, "sub", "col", "row"),
        P(None, "sub", "col"),
    )
    out_specs = P(None, "sub", "col", None)
    return jax.shard_map(
        on_device, mesh=mesh, in_specs=in_specs, out_specs=out_specs, check_vma=False
    )
```
